512 devices in a mesh: dp: 2 (over core), expert: 32 (over z, x), tensor: 8 (over y).
Axes of the slice: x: 4, y: 8, z: 8, core: 2. Of those that a mesh axis runs over, the one named last changes fastest.
Arguments:
- grad_out: bfloat16 [8192, 4096], P(('dp', 'expert'), 'tensor'), may hold values from -6 to 6
- routes: int32 [8192, 8], P(('dp', 'expert')), may hold values from 0 to 31, as said below
- probs: bfloat16 [8192, 8], P(('dp', 'expert')), may hold values from 0.019897461 to 0.25
- vision: int32 [8192], P(('dp', 'expert')), may hold values from 0 to 1, as said below
- pre_text: bfloat16 [2, 32, 2, 32, 28, 1792], P('dp', 'expert', None, None, None, 'tensor'), may hold values from -6 to 6
- pre_vision: bfloat16 [2, 32, 2, 32, 28, 768], P('dp', 'expert', None, None, None, 'tensor'), may hold values from -6 to 6
- down_text: bfloat16 [32, 1792, 4096], P('expert', 'tensor', 'dp'), may hold values from -0.125 to 0.125
- down_vision: bfloat16 [32, 768, 4096], P('expert', 'tensor', 'dp'), may hold values from -0.21875 to 0.21875
Outputs:
- grad_pre_text: bfloat16 [2, 32, 2, 32, 28, 1792], P('dp', 'expert', None, None, None, 'tensor')
- grad_pre_vision: bfloat16 [2, 32, 2, 32, 28, 768], P('dp', 'expert', None, None, None, 'tensor')
- grad_down_text: bfloat16 [32, 1792, 4096], P('expert', 'tensor', 'dp')
- grad_down_vision: bfloat16 [32, 768, 4096], P('expert', 'tensor', 'dp')
- grad_probs: float32 [8192, 8], P(('dp', 'expert'))
The draws below stay inside these ranges and needn't reach their ends.
Inputs may be any that keep to these rules, and one draw needn't show every extreme that they name: `routes`: each row names 8 different ids. Within one block of 128 tokens no id is named by more than 28 tokens of one modality; in each replica one text id and one vision id are named by exactly 28 tokens of that modality in every block of the replica. `vision`: in each block of 128 tokens the image patches form one run, cyclic within the block, of 28 to 100 positions.
All inputs are finite; a program needn't handle non-finite values.
Results may differ from the reference program's by a relative error of at most 0.0059.
Values may be sent and summed in bfloat16 or wider, within the bound.
A program may use at most 128 MiB of HBM per device.

```python
import jax
import jax.numpy as jnp
from jax import lax

D = 4096
FT = 1792
FV = 768
TOPK = 8
TOK_DEV = 128
ET = 32
CAP = 28
TOKENS = 8192
N_DP = 2
N_EXPERT = 32


def route_plan(key):
    block_count = N_DP * N_EXPERT
    keys_all = jax.random.split(key, 6)
    run_length = jax.random.randint(keys_all[0], (block_count, 1), CAP, TOK_DEV - CAP + 1)
    run_start = jax.random.randint(keys_all[1], (block_count, 1), 0, TOK_DEV)
    position = jnp.arange(TOK_DEV, dtype=jnp.int32)[None, :]
    vision = ((position - run_start) % TOK_DEV < run_length).astype(jnp.int32)
    priority = jax.random.randint(keys_all[2], (block_count, TOK_DEV), 0, 1 << 20) * TOK_DEV + position
    same_kind = vision[:, :, None] == vision[:, None, :]
    earlier = priority[:, None, :] < priority[:, :, None]
    kind_rank = jnp.sum((same_kind & earlier).astype(jnp.int32), axis=2)
    hot_pick = jax.random.randint(keys_all[3], (N_DP, 1, 2), 0, ET)
    hot_pick = jnp.broadcast_to(hot_pick, (N_DP, N_EXPERT, 2)).reshape(block_count, 2)
    offsets = jax.random.randint(keys_all[4], (block_count, 2), 0, ET - 1)
    hot_expert = jnp.where(vision == 1, hot_pick[:, 1:2], hot_pick[:, 0:1])
    offset = jnp.where(vision == 1, offsets[:, 1:2], offsets[:, 0:1])
    is_hot = (kind_rank < CAP).astype(jnp.int32)
    stream_base = offset + (TOPK - 1) * jnp.minimum(kind_rank, CAP) + TOPK * jnp.maximum(kind_rank - CAP, 0)
    column = jnp.arange(TOPK, dtype=jnp.int32)
    stream = (stream_base[..., None] + column - is_hot[..., None]) % (ET - 1)
    others = stream + (stream >= hot_expert[..., None]).astype(jnp.int32)
    row_ids = jnp.where((column == 0) & (is_hot[..., None] == 1), hot_expert[..., None], others)
    rotation = jax.random.randint(keys_all[5], (block_count, TOK_DEV, 1), 0, TOPK)
    rotated = (column + rotation) % TOPK
    routes = jnp.take_along_axis(row_ids, rotated, axis=2)
    return (vision.reshape(-1).astype(jnp.int32), routes.reshape(-1, TOPK).astype(jnp.int32))


def draw_routes(key, part):
    return route_plan(key)[1]


def draw_vision(key, part):
    return route_plan(key)[0]


def block_levels(key, extent, cuts, least, top_value):
    loudness, own = 1.0, jax.random.fold_in(key, 6)
    for dim, shards_of in cuts:
        heights = jnp.exp(jax.random.uniform(jax.random.fold_in(own, dim), (shards_of,), jnp.float32, least / len(cuts), top_value / len(cuts)))
        loudness = loudness * jnp.repeat(heights, extent[dim] // shards_of).reshape([-1 if axis == dim else 1 for axis in range(len(extent))])
    return loudness


def scatter_about(own_key, extent, deviation, most, cuts=(), kind=jnp.bfloat16):
    loudness = block_levels(own_key, extent, cuts, -0.22, 0.18) if cuts else 1.0
    array = jax.random.normal(own_key, extent, jnp.float32) * deviation * loudness
    return jnp.minimum(jnp.maximum(array, -most), most).astype(kind)


def setup_inputs(seed: int = 0) -> dict:
    seeds = jax.random.split(jax.random.key(seed), 9)
    return {
        "grad_out": scatter_about(seeds[0], (TOKENS, D), 1.0, 6.0, ((0, 64), (1, 8))),
        "routes": draw_routes(jax.random.fold_in(seeds[8], 71), 0),
        "probs": jnp.clip(0.019897461 + 0.23010254 * jax.random.uniform(seeds[2], (TOKENS, TOPK), jnp.float32) ** block_levels(seeds[2], (TOKENS, TOPK), ((0, 64),), -0.2, 0.2), 0.019897461, 0.25).astype(jnp.bfloat16),
        "vision": draw_vision(jax.random.fold_in(seeds[8], 71), 0),
        "pre_text": scatter_about(seeds[4], (N_DP, ET, 2, N_EXPERT, CAP, FT), 1.0, 6.0, ((0, 2), (1, 32), (5, 8))),
        "pre_vision": scatter_about(seeds[5], (N_DP, ET, 2, N_EXPERT, CAP, FV), 1.0, 6.0, ((0, 2), (1, 32), (5, 8))),
        "down_text": scatter_about(seeds[6], (ET, FT, D), FT ** -0.5, 0.125, ((0, 32), (1, 8), (2, 2))),
        "down_vision": scatter_about(seeds[7], (ET, FV, D), FV ** -0.5, 0.21875, ((0, 32), (1, 8), (2, 2))),
    }


def slot_positions(routes, vision):
    block_count = routes.shape[0] // TOK_DEV
    expert_keys = (routes + ET * vision[:, None]).reshape(block_count, TOK_DEV * TOPK)
    onehot = (expert_keys[:, :, None] == jnp.arange(2 * ET, dtype=jnp.int32)[None, None, :]).astype(jnp.int32)
    before = jnp.cumsum(onehot, axis=1) - onehot
    return jnp.sum(before * onehot, axis=2).reshape(-1).astype(jnp.int32)


def slot_table(routes, vision):
    position = slot_positions(routes, vision)
    pair_index = jnp.arange(TOKENS * TOPK, dtype=jnp.int32)
    token_index = pair_index // TOPK
    block_index = token_index // TOK_DEV
    replica = block_index // N_EXPERT
    sender = block_index % N_EXPERT
    modality = vision[token_index]
    chosen = routes.reshape(-1)
    address = (((replica * 2 + modality) * ET + chosen) * N_EXPERT + sender) * CAP + position
    slot_map = jnp.full((N_DP * 2 * ET * N_EXPERT * CAP,), -1, jnp.int32)
    slot_map = slot_map.at[address.astype(jnp.int32)].set(pair_index)
    return slot_map.reshape(N_DP, 2, ET, N_EXPERT, CAP)


def expert_family(slot_map, grad_out, weights, pre, down):
    def per_expert(expert_id):
        pair_ids = slot_map[:, expert_id]
        present = pair_ids >= 0
        clipped = jnp.maximum(pair_ids, 0)
        slot_rows = jnp.where(present[..., None], grad_out[clipped // TOPK], 0).astype(jnp.bfloat16)
        slot_weight = jnp.where(present, weights[clipped], 0).astype(jnp.float32)
        saved = pre[:, expert_id].astype(jnp.float32)
        gate_pre = saved[:, 0]
        up_pre = saved[:, 1]
        sigmoid_gate = jax.nn.sigmoid(gate_pre)
        hidden = gate_pre * sigmoid_gate * up_pre
        back_grad = jnp.einsum("qscd,fd->qscf", slot_rows.astype(jnp.float32), down[expert_id].astype(jnp.float32))
        scaled = slot_weight[..., None] * back_grad
        grad_gate = scaled * up_pre * sigmoid_gate * (1.0 + gate_pre * (1.0 - sigmoid_gate))
        grad_up = scaled * gate_pre * sigmoid_gate
        grad_pre = jnp.stack([grad_gate, grad_up], axis=1).astype(jnp.bfloat16)
        weighted = (slot_weight[..., None] * hidden).astype(jnp.bfloat16)
        partial_grad = jnp.einsum("qscf,qscd->qfd", weighted.astype(jnp.float32), slot_rows.astype(jnp.float32))
        rounded = lax.optimization_barrier(partial_grad.astype(jnp.bfloat16))
        grad_down = jnp.sum(rounded.astype(jnp.float32), axis=0).astype(jnp.bfloat16)
        score = jnp.sum(hidden * back_grad, axis=-1)
        return grad_pre, grad_down, score

    grad_pre, grad_down, score = lax.map(per_expert, jnp.arange(ET, dtype=jnp.int32))
    return jnp.moveaxis(grad_pre, 0, 1), grad_down, score


def reference(grad_out, routes, probs, vision, pre_text, pre_vision, down_text, down_vision):
    slot_map = slot_table(routes, vision)
    weights = probs.reshape(-1)
    pre_grad_text, down_grad_text, score_text = expert_family(slot_map[:, 0], grad_out, weights, pre_text, down_text)
    pre_grad_vision, down_grad_vision, score_vision = expert_family(slot_map[:, 1], grad_out, weights, pre_vision, down_vision)
    scores = jnp.transpose(jnp.stack([score_text, score_vision], axis=0), (2, 0, 1, 3, 4))
    address = jnp.where(slot_map >= 0, slot_map, TOKENS * TOPK).reshape(-1)
    grad_probs = jnp.zeros((TOKENS * TOPK,), jnp.float32).at[address].set(scores.reshape(-1), mode="drop")
    return pre_grad_text, pre_grad_vision, down_grad_text, down_grad_vision, grad_probs.reshape(TOKENS, TOPK)
```

```python
import functools
import heapq

import jax
import jax.numpy as jnp
from jax import lax
from jax.experimental import pallas as pl
from jax.experimental.pallas import tpu as pltpu
from jax.sharding import PartitionSpec as P

MESH = pl.DeviceIdType.MESH
NL, NS, NT = 8, 4, 8
SLOT = 32
LINKS = ("l+", "l-", "s+", "s-")
SHIFT = {"l+": (0, -1), "l-": (0, 1), "s+": (-1, 0), "s-": (1, 0)}
SIZES = (1.0, 1.0, 1.0, 1.0, 0.125)


def hops(part, ds, dl, via):
    odd = part % 2
    right, left = (4, 3) if odd == 0 else (3, 4)
    up, down = (2, 1) if odd == 0 else (1, 2)
    out = []
    along_l = (via == "l+" and -dl < right) or (via == "l-" and dl < left)
    along_s = (via == "s+" and -ds < up) or (via == "s-" and ds < down)
    if part in (0, 1, 4):
        if dl == 0:
            if ds == 0:
                out += ["s+", "s-"]
            elif along_s:
                out.append(via)
            out += ["l+", "l-"]
        elif along_l:
            out.append(via)
    else:
        if ds == 0:
            if dl == 0:
                out += ["l+", "l-"]
            elif along_l:
                out.append(via)
            out += ["s+", "s-"]
        elif along_s:
            out.append(via)
    return out


def schedule():
    free = {link: 0.0 for link in LINKS}
    queue, count, log = [], 0, []
    for part in (4, 0, 2, 1, 3):
        heapq.heappush(queue, (0.0, count, part, 0, 0, None))
        count += 1
    while queue:
        now, _, part, ds, dl, via = heapq.heappop(queue)
        onward = hops(part, ds, dl, via)
        log.append((part, ds, dl, via, onward))
        for link in onward:
            free[link] = max(now, free[link]) + SIZES[part]
            step_s, step_l = SHIFT[link]
            item = (free[link] + 0.4, count, part, ds + step_s, dl + step_l, link)
            heapq.heappush(queue, item)
            count += 1
    return log


def half_of(t):
    return lax.rem((t + 1) // 2, 2)


def body(
    g_ref, meta_ref, wt_ref, wv_ref, pt_ref, pv_ref,
    gpt_ref, gpv_ref, gdt_ref, gdv_ref, sc_ref,
    buf, bufm, rows_t, rows_v, wtb, wvb, hid_t, hid_v, phid_t, phid_v,
    wgt_t, wgt_v, bown_t, bown_v, bsend_t, bsend_v, brecv_t, brecv_v,
    acc_t, acc_v, give_t, give_v, grecv_t, grecv_v, res_t, res_v,
    sel, sw, tmp_t, tmp_v,
    ysend, yrecv, csend, crecv, wsend, wrecv, hsend, hrecv, bsem, brsem,
    gsend, grsem, fsend, frecv,
):
    f32, bf16 = jnp.float32, jnp.bfloat16
    q = lax.axis_index("dp")
    e = lax.axis_index("expert")
    t = lax.axis_index("tensor")
    zl, xs = e // NS, lax.rem(e, NS)
    pair = t + 1 - 2 * lax.rem(t, 2)
    other = 1 - q
    mine = half_of(t)
    main = q == mine

    def chip(s_, l_):
        return lax.rem(l_ + 2 * NL, NL) * NS + lax.rem(s_ + 2 * NS, NS)

    near = {
        "l+": chip(xs, zl + 1), "l-": chip(xs, zl - 1),
        "s+": chip(xs + 1, zl), "s-": chip(xs - 1, zl),
    }

    barrier = pltpu.get_barrier_semaphore()
    for link in LINKS:
        pl.semaphore_signal(barrier, inc=1, device_id=(q, near[link], t), device_id_type=MESH)
    for k in range(1, NT):
        pl.semaphore_signal(
            barrier, inc=1, device_id=(q, e, lax.rem(t + k, NT)), device_id_type=MESH
        )
    pl.semaphore_signal(barrier, inc=1, device_id=(other, e, t), device_id_type=MESH)
    pl.semaphore_signal(barrier, inc=1, device_id=(other, e, pair), device_id_type=MESH)
    pl.semaphore_wait(barrier, 4 + NT - 1 + 2)

    def remote(src, dst, send, recv, where):
        return pltpu.make_async_remote_copy(
            src_ref=src, dst_ref=dst, send_sem=send, recv_sem=recv,
            device_id=where, device_id_type=MESH,
        )

    slice_id = lax.rem(t, 4)
    late = t // 4

    def taker(i):
        return (i // 2) * 4 + jnp.where(late == 0, 3 * (i % 2), 1 + (i % 2))

    for i in range(4):
        copy = remote(
            g_ref, buf.at[e, slice_id], ysend.at[i], yrecv.at[slice_id], (q, e, taker(i))
        )

        @pl.when(taker(i) != t)
        def _():
            copy.start()

        @pl.when(taker(i) == t)
        def _():
            pltpu.make_async_copy(g_ref, buf.at[e, slice_id], yrecv.at[slice_id]).start()

    keep = pltpu.make_async_copy(meta_ref, bufm.at[e], crecv.at[4, 0])
    keep.start()

    tmp_t[...] = jnp.zeros_like(tmp_t)
    tmp_v[...] = jnp.zeros_like(tmp_v)

    def pieces(ref, s):
        gate = ref[0, 0, 0, s].astype(f32)
        up = ref[0, 0, 1, s].astype(f32)
        sig = jax.nn.sigmoid(gate)
        return gate, up, sig

    def hidden_step(s, carry):
        for ref, tmp, hid in ((pt_ref, tmp_t, hid_t), (pv_ref, tmp_v, hid_v)):
            gate, up, sig = pieces(ref, s)
            tmp[0:28, :] = gate * sig * up
            hid[s] = tmp[...].astype(bf16)
        return carry

    lax.fori_loop(0, 32, hidden_step, 0)

    log = schedule()
    done_at = {}
    for n, (part, ds, dl, via, onward) in enumerate(log):
        dist = min(dl % NL, (-dl) % NL)
        done_at[dist] = n
    sent = {link: 0 for link in LINKS}
    sends = []
    later = []

    def at(part, src):
        return bufm.at[src] if part == 4 else buf.at[src, part]

    def early_sends():
        for k, (mine_ref, box) in enumerate(((hid_t, phid_t), (hid_v, phid_v))):
            copy = remote(mine_ref, box, hsend.at[k], hrecv.at[k], (q, e, pair))
            copy.start()
            later.append(copy)
        for k, (src, box) in enumerate(((wt_ref, wtb), (wv_ref, wvb))):
            @pl.when(main)
            def _():
                pltpu.make_async_copy(src.at[0], box.at[0], wrecv.at[0, k]).start()
                remote(
                    src.at[0], box.at[0], wsend.at[0, k], wrecv.at[0, k], (other, e, t)
                ).start()

            @pl.when(jnp.logical_not(main))
            def _():
                remote(
                    src.at[0], box.at[1], wsend.at[0, k], wrecv.at[1, k], (other, e, pair)
                ).start()
                remote(
                    src.at[0], box.at[1], wsend.at[1, k], wrecv.at[1, k], (q, e, pair)
                ).start()

    upper = (
        lax.broadcasted_iota(jnp.int32, (128, 128), 0)
        < lax.broadcasted_iota(jnp.int32, (128, 128), 1)
    ).astype(bf16)

    def block_of(dist, i):
        sign = 1 - 2 * (i // 4)
        return chip(xs + lax.rem(i, 4), zl + dist * sign)

    def gather_block(dist, i):
        src = block_of(dist, i)
        table = bufm[src].astype(f32)
        row = lax.broadcasted_iota(jnp.int32, (16, 512), 0)
        found = []
        for family in range(2):
            line = jnp.sum(
                jnp.where(row == family * 8 + e // 4, table, 0.0), axis=0, keepdims=True
            )
            w = jnp.zeros((1, 128), f32)
            for k in range(4):
                w = jnp.where(lax.rem(e, 4) == k, line[:, k * 128 : (k + 1) * 128], w)
            found.append(w)
        sub = lax.broadcasted_iota(jnp.int32, (8, 128), 0)
        both = jnp.where(sub == 0, found[0], jnp.where(sub == 1, found[1], 0.0))
        match = (both > 0.0).astype(bf16)
        rank = jnp.dot(match, upper, preferred_element_type=f32)
        want = lax.broadcasted_iota(jnp.int32, (SLOT, 128), 0).astype(f32)
        picks = []
        for family in range(2):
            w = found[family]
            hit = jnp.logical_and(want == rank[family : family + 1], w > 0.0)
            pick = jnp.where(hit, 1.0, 0.0)
            sw[family, src] = jnp.broadcast_to(
                jnp.sum(pick * w, axis=1, keepdims=True), (SLOT, 128)
            )
            picks.append(pick)
        pick = jnp.concatenate(picks, axis=0).astype(bf16)
        sel[src] = pick
        spot = pl.ds(pl.multiple_of(i * SLOT, SLOT), SLOT)
        for part in range(4):
            got = jnp.dot(pick, buf[src, part], preferred_element_type=f32).astype(bf16)
            cols = slice(part * 512, (part + 1) * 512)
            rows_t[spot, cols] = got[0:SLOT]
            rows_v[spot, cols] = got[SLOT : 2 * SLOT]
        for family, (wgt, own, their) in enumerate(
            ((wgt_t, hid_t, phid_t), (wgt_v, hid_v, phid_v))
        ):
            scale = sw[family, src][:, 0:1]
            wgt[0, spot] = (scale * own[src].astype(f32)).astype(bf16)
            wgt[1, spot] = (scale * their[src].astype(f32)).astype(bf16)

    start_of = {0: 0, 1: 128, 2: 384, 3: 640, 4: 896}
    families = (
        (rows_t, wtb, wgt_t, bown_t, bsend_t, brecv_t, acc_t),
        (rows_v, wvb, wgt_v, bown_v, bsend_v, brecv_v, acc_v),
    )

    def exchange(dist, k):
        m = 128 if dist in (0, 4) else 256
        rows = pl.ds(start_of[dist], m)
        fam = families[k]
        return remote(
            fam[4].at[rows], fam[5].at[rows], bsem.at[dist, k], brsem.at[dist, k], (q, e, pair)
        )

    def update(dist, part):
        m = 128 if dist in (0, 4) else 256
        cols = slice(part * 512, (part + 1) * 512)
        for rows, _, wgt, _, _, _, acc in families:
            for k in range(2):
                add = lax.dot_general(
                    wgt[k, 0:m], rows[0:m, cols], (((0,), (0,)), ((), ())),
                    preferred_element_type=f32,
                )
                if dist == 0:
                    acc[k, :, cols] = add
                else:
                    acc[k, :, cols] += add

    def work(dist):
        count = 4 if dist in (0, 4) else 8
        m = count * SLOT

        def step(i, carry):
            gather_block(dist, i)
            return carry

        lax.fori_loop(0, count, step, 0)
        base = start_of[dist]
        for k, (rows, wb, _, bown, bsend, _, _) in enumerate(families):
            nt = (((1,), (1,)), ((), ()))
            bsend[base : base + m] = lax.dot_general(
                rows[0:m], wb[1], nt, preferred_element_type=f32
            ).astype(bf16)
            exchange(dist, k).start()
        for k, (rows, wb, _, bown, bsend, _, _) in enumerate(families):
            nt = (((1,), (1,)), ((), ()))
            bown[base : base + m] = lax.dot_general(
                rows[0:m], wb[0], nt, preferred_element_type=f32
            )

    def finish(dist):
        count = 4 if dist in (0, 4) else 8
        for k in range(2):
            exchange(dist, k).wait()

        def step(i, carry):
            src = block_of(dist, i)
            spot = pl.ds(pl.multiple_of(start_of[dist] + i * SLOT, SLOT), SLOT)
            total = jnp.zeros((1, 128), f32)
            for family, (ref, out, bown, brecv) in enumerate(
                ((pt_ref, gpt_ref, bown_t, brecv_t), (pv_ref, gpv_ref, bown_v, brecv_v))
            ):
                back = (bown[spot] + brecv[spot].astype(f32))[0:28]
                gate, up, sig = pieces(ref, src)
                scaled = sw[family, src][0:28, 0:1] * back
                out[0, 0, 0, src] = (scaled * up * sig * (1.0 + gate * (1.0 - sig))).astype(bf16)
                out[0, 0, 1, src] = (scaled * gate * sig).astype(bf16)
                score = jnp.sum(gate * sig * up * back, axis=1, keepdims=True)
                pick = sel[src, family * SLOT : family * SLOT + SLOT].astype(f32)
                total += jnp.sum(pick[0:28] * score, axis=0, keepdims=True)
            sc_ref[pl.ds(src, 1), :] = total
            return carry

        lax.fori_loop(0, count, step, 0)

    waited_early = False
    for n, (part, ds, dl, via, onward) in enumerate(log):
        src = chip(xs + ds, zl + dl)
        if via is None:
            if part == 4:
                keep.wait()
            else:
                pltpu.make_async_copy(g_ref, buf.at[e, part], yrecv.at[part]).wait()
        else:
            here = at(part, src)
            pltpu.make_async_copy(here, here, crecv.at[part, (ds % NS) * NL + dl % NL]).wait()
        for link in onward:
            step_s, step_l = SHIFT[link]
            spot = ((ds + step_s) % NS) * NL + (dl + step_l) % NL
            copy = remote(
                at(part, src), at(part, src), csend.at[LINKS.index(link), sent[link]],
                crecv.at[part, spot], (q, near[link], t),
            )
            copy.start()
            sent[link] += 1
            sends.append(copy)
        if n == 4:
            early_sends()
        for dist in range(5):
            if done_at[dist] == n:
                if dist == 0:
                    for k, (mine_ref, box) in enumerate(((hid_t, phid_t), (hid_v, phid_v))):
                        later[k].wait_recv()
                    for k, (src_w, box) in enumerate(((wt_ref, wtb), (wv_ref, wvb))):
                        for slot in range(2):
                            pltpu.make_async_copy(
                                src_w.at[0], box.at[slot], wrecv.at[slot, k]
                            ).wait()
                work(dist)
                if dist < 4:
                    for part_ in range(4):
                        update(dist, part_)
                if dist > 0:
                    finish(dist - 1)

    chosen = jnp.where(main, 0, 1)
    given = 1 - chosen
    outs = ((acc_t, give_t, grecv_t, res_t, gdt_ref), (acc_v, give_v, grecv_v, res_v, gdv_ref))

    def hand(part, k):
        _, give, grecv, _, _ = outs[k]
        return remote(
            give.at[part], grecv.at[part], gsend.at[part, k], grsem.at[part, k], (other, e, t)
        )

    def forward(part, k):
        _, _, _, res, out = outs[k]
        cols = pl.ds(part * 512, 512)
        return remote(
            res.at[part], out.at[0, :, cols], fsend.at[part, k], frecv.at[part, k],
            (other, e, pair),
        )

    def add_up(part):
        cols = slice(part * 512, (part + 1) * 512)
        for k, (acc, give, grecv, res, out) in enumerate(outs):
            hand(part, k).wait_recv()
            here = acc[chosen, :, cols].astype(bf16).astype(f32)
            total = (here + grecv[part].astype(f32)).astype(bf16)

            @pl.when(main)
            def _():
                out[0, :, cols] = total

            @pl.when(jnp.logical_not(main))
            def _():
                res[part] = total
                forward(part, k).start()

    for part in range(4):
        update(4, part)
        cols = slice(part * 512, (part + 1) * 512)
        for k, (acc, give, grecv, res, out) in enumerate(outs):
            give[part] = acc[given, :, cols].astype(bf16)
            hand(part, k).start()
        if part > 0:
            add_up(part - 1)
    add_up(3)
    finish(4)

    for copy in sends:
        copy.wait_send()
    for copy in later:
        copy.wait_send()
    for part in range(4):
        for k in range(2):
            hand(part, k).wait_send()

            @pl.when(jnp.logical_not(main))
            def _():
                forward(part, k).wait()
    for k, (src, box) in enumerate(((wt_ref, wtb), (wv_ref, wvb))):
        pltpu.make_async_copy(src.at[0], box.at[0], wsend.at[0, k]).wait()

        @pl.when(jnp.logical_not(main))
        def _():
            pltpu.make_async_copy(src.at[0], box.at[0], wsend.at[1, k]).wait()

    for i in range(4):
        @pl.when(taker(i) != t)
        def _():
            pltpu.make_async_copy(g_ref, g_ref, ysend.at[i]).wait()


def owner_kernel(grad_out, meta, down_text, down_vision, pre_text, pre_vision):
    f32, bf16 = jnp.float32, jnp.bfloat16
    ft, fv = pre_text.shape[-1], pre_vision.shape[-1]
    vmem = pl.BlockSpec(memory_space=pltpu.VMEM)
    dma = pltpu.SemaphoreType.DMA
    like = jax.ShapeDtypeStruct
    return pl.pallas_call(
        body,
        out_shape=(
            like(pre_text.shape, bf16), like(pre_vision.shape, bf16),
            like(down_text.shape, bf16), like(down_vision.shape, bf16),
            like((32, 128), f32),
        ),
        in_specs=[vmem] * 6,
        out_specs=(vmem,) * 5,
        scratch_shapes=[
            pltpu.VMEM((32, 4, 128, 512), bf16), pltpu.VMEM((32, 16, 512), bf16),
            pltpu.VMEM((256, 2048), bf16), pltpu.VMEM((256, 2048), bf16),
            pltpu.VMEM((2, ft, 2048), bf16), pltpu.VMEM((2, fv, 2048), bf16),
            pltpu.VMEM((32, SLOT, ft), bf16), pltpu.VMEM((32, SLOT, fv), bf16),
            pltpu.VMEM((32, SLOT, ft), bf16), pltpu.VMEM((32, SLOT, fv), bf16),
            pltpu.VMEM((2, 256, ft), bf16), pltpu.VMEM((2, 256, fv), bf16),
            pltpu.VMEM((1024, ft), f32), pltpu.VMEM((1024, fv), f32),
            pltpu.VMEM((1024, ft), bf16), pltpu.VMEM((1024, fv), bf16),
            pltpu.VMEM((1024, ft), bf16), pltpu.VMEM((1024, fv), bf16),
            pltpu.VMEM((2, ft, 2048), f32), pltpu.VMEM((2, fv, 2048), f32),
            pltpu.VMEM((4, ft, 512), bf16), pltpu.VMEM((4, fv, 512), bf16),
            pltpu.VMEM((4, ft, 512), bf16), pltpu.VMEM((4, fv, 512), bf16),
            pltpu.VMEM((4, ft, 512), bf16), pltpu.VMEM((4, fv, 512), bf16),
            pltpu.VMEM((32, 2 * SLOT, 128), bf16), pltpu.VMEM((2, 32, SLOT, 128), f32),
            pltpu.VMEM((SLOT, ft), f32), pltpu.VMEM((SLOT, fv), f32),
            dma((4,)), dma((4,)), dma((4, 56)), dma((5, 32)),
            dma((2, 2)), dma((2, 2)), dma((2,)), dma((2,)), dma((5, 2)), dma((5, 2)),
            dma((4, 2)), dma((4, 2)), dma((4, 2)), dma((4, 2)),
        ],
        compiler_params=pltpu.CompilerParams(
            collective_id=0, has_side_effects=True, vmem_limit_bytes=60 * 1024 * 1024
        ),
        cost_estimate=pl.CostEstimate(
            flops=7_000_000_000, bytes_accessed=10_000_000, transcendentals=2_000_000
        ),
    )(grad_out, meta, down_text, down_vision, pre_text, pre_vision)


def on_device(grad_out, routes, probs, vision, pre_text, pre_vision, down_text, down_vision):
    experts = jnp.arange(32, dtype=jnp.int32)
    hit = routes[None, :, :] == experts[:, None, None]
    weight = jnp.sum(jnp.where(hit, probs[None].astype(jnp.float32), 0.0), axis=2)
    meta = jnp.concatenate(
        [jnp.where(vision == 0, weight, 0.0), jnp.where(vision == 1, weight, 0.0)], axis=0
    )
    meta = meta.astype(jnp.bfloat16).reshape(16, 512)
    gpt, gpv, gdt, gdv, score = owner_kernel(
        grad_out, meta, down_text, down_vision, pre_text, pre_vision
    )
    score = lax.psum(score, "tensor")
    back = lax.all_to_all(score, "expert", split_axis=0, concat_axis=0, tiled=True)
    grad_probs = jnp.sum(jnp.where(hit, back[:, :, None], 0.0), axis=0)
    return gpt, gpv, gdt, gdv, grad_probs


def solution(mesh):
    in_specs = (
        P(("dp", "expert"), "tensor"),
        P(("dp", "expert"), None),
        P(("dp", "expert"), None),
        P(("dp", "expert")),
        P("dp", "expert", None, None, None, "tensor"),
        P("dp", "expert", None, None, None, "tensor"),
        P("expert", "tensor", "dp"),
        P("expert", "tensor", "dp"),
    )
    out_specs = (
        P("dp", "expert", None, None, None, "tensor"),
        P("dp", "expert", None, None, None, "tensor"),
        P("expert", "tensor", "dp"),
        P("expert", "tensor", "dp"),
        P(("dp", "expert"), None),
    )
    return jax.shard_map(
        on_device, mesh=mesh, in_specs=in_specs, out_specs=out_specs, check_vma=False
    )
```

```python
import heapq

import jax
import jax.numpy as jnp
from jax import lax
from jax.experimental import pallas as pl
from jax.experimental.pallas import tpu as pltpu
from jax.sharding import PartitionSpec as P

MESH = pl.DeviceIdType.MESH
NL, NS, NT = 8, 4, 8
SLOT = 32
CAP = 28
LINKS = ("l+", "l-", "s+", "s-")
SHIFT = {"l+": (0, -1), "l-": (0, 1), "s+": (-1, 0), "s-": (1, 0)}
META = 3
CHUNKS = (
    (META, "s", 0, (0, 64), (0, 128), 0.0),
    (0, "s", 0, (0, 48), (0, 512), 0.0),
    (0, "l", 1, (48, 128), (0, 512), 0.0),
    (1, "s", 1, (0, 48), (0, 512), 3.0),
    (1, "l", 0, (48, 128), (0, 512), 3.0),
    (2, "s", 0, (0, 48), (0, 256), 4.5),
    (2, "s", 1, (0, 48), (256, 512), 4.5),
    (2, "l", 0, (48, 128), (0, 256), 4.5),
    (2, "l", 1, (48, 128), (256, 512), 4.5),
)
FIRST_TASK = 9.0
DELAY = 14
GROUPS = 5
BASE = {0: 0, 1: 128, 2: 384, 3: 640, 4: 896}
BLOCKS = {0: 4, 1: 8, 2: 8, 3: 8, 4: 4}


def hops(first, odd, ds, dl, via):
    right, left = (4, 3) if odd == 0 else (3, 4)
    up, down = (2, 1) if odd == 0 else (1, 2)
    out = []
    along_l = (via == "l+" and -dl < right) or (via == "l-" and dl < left)
    along_s = (via == "s+" and -ds < up) or (via == "s-" and ds < down)
    if first == "s":
        if dl == 0:
            if ds == 0:
                out += ["s+", "s-"]
            elif along_s:
                out.append(via)
            out += ["l+", "l-"]
        elif along_l:
            out.append(via)
    else:
        if ds == 0:
            if dl == 0:
                out += ["l+", "l-"]
            elif along_l:
                out.append(via)
            out += ["s+", "s-"]
        elif along_s:
            out.append(via)
    return out


def schedule():
    free = {link: 0.0 for link in LINKS}
    queue, count, log = [], 0, []
    for c, chunk in enumerate(CHUNKS):
        heapq.heappush(queue, (chunk[5], count, c, 0, 0, None))
        count += 1
    while queue:
        now, _, c, ds, dl, via = heapq.heappop(queue)
        _, first, odd, rows, cols, _ = CHUNKS[c]
        size = (rows[1] - rows[0]) * (cols[1] - cols[0]) / (128 * 512)
        onward = hops(first, odd, ds, dl, via)
        log.append((now, c, ds, dl, via, onward))
        for link in onward:
            free[link] = max(now, free[link]) + size
            step_s, step_l = SHIFT[link]
            item = (free[link] + 0.4, count, c, ds + step_s, dl + step_l, link)
            heapq.heappush(queue, item)
            count += 1
    return log


def slice_of(j, t):
    odd = lax.rem(t, 2)
    mate = lax.rem(t + NT + 2 * odd - 1, NT)
    if j == 0:
        return t
    if j == 1:
        return lax.rem(t + NT + 3 - 6 * odd, NT)
    if j == 2:
        return slice_of(1, mate)
    return mate


def body(
    g_ref, routes_ref, probs_ref, vision_ref, wt_ref, wv_ref, pt_ref, pv_ref,
    gpt_ref, gpv_ref, gdt_ref, gdv_ref, gp_ref,
    buf, bufm, rows_t, rows_v, srow_t, srow_v, prow_t, prow_v, wb_t, wb_v,
    wgt_t, wgt_v, pwgt_t, pwgt_v, bown_t, bown_v, bpair_t, bpair_v,
    bsend_t, bsend_v, brecv_t, brecv_v, acc_t, acc_v, give_t, give_v,
    grecv_t, grecv_v, res_t, res_v, sel, sw, tmp_t, tmp_v, scs, p1, scin, gall,
    ysend, yrecv, csend, crecv, wsend, wrecv, wback, hsend, hrecv, rsend, rrecv,
    bsem, brsem, gsend, grsem, fsend, frecv, s1send, s1recv, s2send, s2recv,
    tsend, trecv,
):
    f32, bf16 = jnp.float32, jnp.bfloat16
    q = lax.axis_index("dp")
    e = lax.axis_index("expert")
    t = lax.axis_index("tensor")
    zl, xs = e // NS, lax.rem(e, NS)
    pair = t + 1 - 2 * lax.rem(t, 2)
    mate = slice_of(3, t)
    far = slice_of(1, t)
    other = 1 - q

    def chip(s_, l_):
        return lax.rem(l_ + 2 * NL, NL) * NS + lax.rem(s_ + 2 * NS, NS)

    near = {
        "l+": chip(xs, zl + 1), "l-": chip(xs, zl - 1),
        "s+": chip(xs + 1, zl), "s-": chip(xs - 1, zl),
    }

    barrier = pltpu.get_barrier_semaphore()

    def greet(where):
        pl.semaphore_signal(barrier, inc=1, device_id=where, device_id_type=MESH)

    for k in range(1, NL):
        greet((q, chip(xs, zl + k), t))
    for k in range(1, NS):
        greet((q, chip(xs + k, zl), t))
    for k in range(1, NT):
        greet((q, e, lax.rem(t + k, NT)))
    greet((other, e, t))
    pl.semaphore_wait(barrier, NL + NS + NT - 3 + 1)

    def remote(src, dst, send, recv, where):
        return pltpu.make_async_remote_copy(
            src_ref=src, dst_ref=dst, send_sem=send, recv_sem=recv,
            device_id=where, device_id_type=MESH,
        )

    def arrived(ref, sem):
        pltpu.make_async_copy(ref, ref, sem).wait()

    y_copies = (
        remote(g_ref, buf.at[1, e], ysend.at[0], yrecv.at[0], (q, e, far)),
        remote(buf.at[1, e], buf.at[2, e], ysend.at[1], yrecv.at[1], (q, e, mate)),
    )
    y_copies[0].start()
    own = pltpu.make_async_copy(g_ref, buf.at[0, e], yrecv.at[2])
    own.start()

    expert = lax.broadcasted_iota(jnp.int32, (32, 128), 0)
    weight = jnp.zeros((32, 128), f32)
    for k in range(8):
        named = routes_ref[k : k + 1, :] == expert
        weight += jnp.where(named, probs_ref[k : k + 1, :], 0.0)
    image = vision_ref[...] == 1
    bufm[e, 0:32] = jnp.where(image, 0.0, weight).astype(bf16)
    bufm[e, 32:64] = jnp.where(image, weight, 0.0).astype(bf16)
    tmp_t[...] = jnp.zeros_like(tmp_t)
    tmp_v[...] = jnp.zeros_like(tmp_v)
    own.wait()

    w_fams = ((wt_ref, wb_t), (wv_ref, wb_v))

    def w_cols(u):
        return pl.ds(pl.multiple_of(lax.rem(u, 4) * 512, 512), 512)

    def w_copies(j, k, action):
        src, box = w_fams[k]
        u = slice_of(j, t)
        v = slice_of(j, pair)

        @pl.when(u // 4 == q)
        def _():
            here = src.at[0, :, w_cols(u)]
            there = remote(here, box.at[0, j], wsend.at[0, j, k], wrecv.at[0, j, k], (other, e, t))
            if action == "start":
                pltpu.make_async_copy(here, box.at[0, j], wrecv.at[0, j, k]).start()
                there.start()
            else:
                there.wait_send()

        @pl.when(v // 4 == q)
        def _():
            there = remote(
                src.at[0, :, w_cols(v)], box.at[1, j], wsend.at[1, j, k], wrecv.at[1, j, k],
                (q, e, pair),
            )
            if action == "start":
                there.start()
            else:
                there.wait_send()

    def w_relay(j, k):
        box = w_fams[k][1]
        return remote(
            box.at[1, j], box.at[1, j], wback.at[j, k], wrecv.at[1, j, k], (other, e, t)
        )

    def w_arrive():
        for j in range(4):
            for k in range(2):
                arrived(w_fams[k][1].at[1, j], wrecv.at[1, j, k])

                @pl.when(slice_of(j, t) // 4 == q)
                def _():
                    w_relay(j, k).start()

        for j in range(4):
            for k in range(2):
                arrived(w_fams[k][1].at[0, j], wrecv.at[0, j, k])

    def w_relayed():
        for j in range(4):
            for k in range(2):
                @pl.when(slice_of(j, t) // 4 == q)
                def _():
                    w_relay(j, k).wait_send()

    upper = (
        lax.broadcasted_iota(jnp.int32, (128, 128), 0)
        < lax.broadcasted_iota(jnp.int32, (128, 128), 1)
    ).astype(bf16)

    def block_of(g, i):
        sign = 1 - 2 * (i // 4)
        return chip(xs + lax.rem(i, 4), zl + g * sign)

    def place(g, i):
        return pl.ds(pl.multiple_of(BASE[g] + i * SLOT, SLOT), SLOT)

    def span(g):
        return slice(BASE[g], BASE[g] + BLOCKS[g] * SLOT)

    def pieces(ref, s):
        gate = ref[0, 0, 0, s].astype(f32)
        up = ref[0, 0, 1, s].astype(f32)
        return gate, up, jax.nn.sigmoid(gate)

    fams = (
        dict(pre=pt_ref, grad=gpt_ref, rows=rows_t, srow=srow_t, prow=prow_t, wb=wb_t, wgt=wgt_t,
             pwgt=pwgt_t, bown=bown_t, bpair=bpair_t, bsend=bsend_t, brecv=brecv_t, acc=acc_t,
             give=give_t, grecv=grecv_t, res=res_t, out=gdt_ref, tmp=tmp_t),
        dict(pre=pv_ref, grad=gpv_ref, rows=rows_v, srow=srow_v, prow=prow_v, wb=wb_v, wgt=wgt_v,
             pwgt=pwgt_v, bown=bown_v, bpair=bpair_v, bsend=bsend_v, brecv=brecv_v, acc=acc_v,
             give=give_v, grecv=grecv_v, res=res_v, out=gdv_ref, tmp=tmp_v),
    )

    def wgt_copy(g, k):
        at = pl.ds(BASE[g], BLOCKS[g] * SLOT)
        return remote(
            fams[k]["wgt"].at[at], fams[k]["pwgt"].at[at], hsend.at[g, k], hrecv.at[g, k],
            (q, e, pair),
        )

    def prepare(g):
        def step(i, carry):
            src = block_of(g, i)
            table = bufm[src].astype(f32)
            row = lax.broadcasted_iota(jnp.int32, (64, 128), 0)
            found = [
                jnp.sum(jnp.where(row == k * 32 + e, table, 0.0), axis=0, keepdims=True)
                for k in range(2)
            ]
            sub = lax.broadcasted_iota(jnp.int32, (8, 128), 0)
            both = jnp.where(sub == 0, found[0], jnp.where(sub == 1, found[1], 0.0))
            rank = jnp.dot((both > 0.0).astype(bf16), upper, preferred_element_type=f32)
            want = lax.broadcasted_iota(jnp.int32, (SLOT, 128), 0).astype(f32)
            for k, fam in enumerate(fams):
                hit = jnp.logical_and(want == rank[k : k + 1], found[k] > 0.0)
                pick = jnp.where(hit, 1.0, 0.0)
                scale = jnp.sum(pick * found[k], axis=1, keepdims=True)
                sw[k, src] = jnp.broadcast_to(scale, (SLOT, 128))
                sel[src, k * SLOT : (k + 1) * SLOT] = pick.astype(bf16)
                gate, up, sig = pieces(fam["pre"], src)
                fam["tmp"][0:CAP, :] = gate * sig * up
                fam["wgt"][place(g, i)] = (scale * fam["tmp"][...]).astype(bf16)
            return carry

        lax.fori_loop(0, BLOCKS[g], step, 0)
        for k in range(2):
            wgt_copy(g, k).start()

    def row_copy(g, k):
        at = pl.ds(BASE[g], BLOCKS[g] * SLOT)
        return remote(
            fams[k]["srow"].at[at], fams[k]["prow"].at[at], rsend.at[g, k], rrecv.at[g, k],
            (q, e, mate),
        )

    def back_copy(g, k):
        at = pl.ds(BASE[g], BLOCKS[g] * SLOT)
        return remote(
            fams[k]["bsend"].at[at], fams[k]["brecv"].at[at], bsem.at[g, k], brsem.at[g, k],
            (q, e, pair),
        )

    nt_dims = (((1,), (1,)), ((), ()))
    tn_dims = (((0,), (0,)), ((), ()))
    waited = set()
    begun = set()
    added = {g: 0 for g in range(GROUPS)}

    def select(j, g):
        def step(i, carry):
            src = block_of(g, i)
            got = jnp.dot(sel[src], buf[j, src], preferred_element_type=f32).astype(bf16)
            for k, fam in enumerate(fams):
                if j == 0:
                    fam["srow"][place(g, i)] = got[k * SLOT : (k + 1) * SLOT]
                else:
                    spot = pl.ds(pl.multiple_of(i * SLOT, SLOT), SLOT)
                    fam["rows"][spot] = got[k * SLOT : (k + 1) * SLOT]
            return carry

        lax.fori_loop(0, BLOCKS[g], step, 0)
        if j == 0:
            for k in range(2):
                row_copy(g, k).start()

    def products(j, g):
        m = BLOCKS[g] * SLOT
        if g not in waited:
            waited.add(g)
            for k in range(2):
                wgt_copy(g, k).wait_recv()
        if j == 3:
            for k in range(2):
                row_copy(g, k).wait_recv()
        final = added[g] == 3
        for k, fam in enumerate(fams):
            rows = {0: fam["srow"], 3: fam["prow"]}.get(j)
            rows = fam["rows"][0:m] if rows is None else rows[span(g)]
            theirs = lax.dot_general(rows, fam["wb"][1, j], nt_dims, preferred_element_type=f32)
            if added[g]:
                theirs += fam["bpair"][span(g)]
            if final:
                fam["bsend"][span(g)] = theirs.astype(bf16)
                back_copy(g, k).start()
            else:
                fam["bpair"][span(g)] = theirs
        for k, fam in enumerate(fams):
            rows = {0: fam["srow"], 3: fam["prow"]}.get(j)
            rows = fam["rows"][0:m] if rows is None else rows[span(g)]
            ours = lax.dot_general(rows, fam["wb"][0, j], nt_dims, preferred_element_type=f32)
            if added[g]:
                ours += fam["bown"][span(g)]
            fam["bown"][span(g)] = ours
            for n, wgt in enumerate((fam["wgt"], fam["pwgt"])):
                add = lax.dot_general(wgt[span(g)], rows, tn_dims, preferred_element_type=f32)
                if j in begun:
                    fam["acc"][n, j] += add
                else:
                    fam["acc"][n, j] = add
        added[g] += 1
        begun.add(j)
        return final

    def hand(j, k):
        fam = fams[k]
        return remote(
            fam["give"].at[j], fam["grecv"].at[j], gsend.at[j, k], grsem.at[j, k], (other, e, t)
        )

    def forward(j, k):
        fam = fams[k]
        return remote(
            fam["res"].at[j], fam["out"].at[0, :, w_cols(slice_of(j, t))], fsend.at[j, k],
            frecv.at[j, k], (q, e, pair),
        )

    def give_away(j):
        @pl.when(slice_of(j, t) // 4 != q)
        def _():
            for k, fam in enumerate(fams):
                fam["give"][j] = fam["acc"][:, j].astype(bf16)
                hand(j, k).start()

    def add_up(j):
        @pl.when(slice_of(j, t) // 4 == q)
        def _():
            for k, fam in enumerate(fams):
                hand(j, k).wait_recv()
                for n in (1, 0):
                    here = fam["acc"][n, j].astype(bf16).astype(f32)
                    total = (here + fam["grecv"][j, n].astype(f32)).astype(bf16)
                    if n == 1:
                        fam["res"][j] = total
                        forward(j, k).start()
                    else:
                        fam["out"][0, :, w_cols(slice_of(j, t))] = total

    def score_copy(g, sign):
        to = lax.rem(zl + sign * g + NL, NL)
        return remote(
            scs.at[pl.ds(to * NS, NS)], p1.at[:, zl], s1send.at[(sign * g) % NL],
            s1recv.at[(-sign * g) % NL], (q, chip(xs, zl + sign * g), t),
        )

    def finish(g):
        for k in range(2):
            back_copy(g, k).wait_recv()

        def step(i, carry):
            src = block_of(g, i)
            total = jnp.zeros((1, 128), f32)
            for k, fam in enumerate(fams):
                spot = place(g, i)
                back = (fam["bown"][spot] + fam["brecv"][spot].astype(f32))[0:CAP]
                gate, up, sig = pieces(fam["pre"], src)
                scaled = sw[k, src][0:CAP, 0:1] * back
                grad = fam["grad"]
                grad[0, 0, 0, src] = (scaled * up * sig * (1.0 + gate * (1.0 - sig))).astype(bf16)
                grad[0, 0, 1, src] = (scaled * gate * sig).astype(bf16)
                score = jnp.sum(gate * sig * up * back, axis=1, keepdims=True)
                pick = sel[src, k * SLOT : (k + 1) * SLOT].astype(f32)
                total += jnp.sum(pick[0:CAP] * score, axis=0, keepdims=True)
            scs[src] = total
            return carry

        lax.fori_loop(0, BLOCKS[g], step, 0)
        if g == 0:
            p1[:, zl] = scs[pl.ds(zl * NS, NS)]
        elif g == 4:
            score_copy(4, 1).start()
        else:
            score_copy(g, 1).start()
            score_copy(g, -1).start()

    log = schedule()
    ready = {}
    for n, (now, c, ds, dl, via, onward) in enumerate(log):
        ready[(CHUNKS[c][0], min(dl % NL, -dl % NL))] = n
    sent = {link: 0 for link in LINKS}
    sends = []
    todo = []
    groups_left = {j: GROUPS for j in range(4)}

    def plan(n, needs, call):
        todo.append((n, len(todo) + planned[0], needs, call))
        planned[0] += 1
        todo.sort(key=lambda item: item[:2])

    planned = [0]

    def multiply(n, j, g):
        if products(j, g):
            plan(n + DELAY, False, lambda m: finish(g))
        groups_left[j] -= 1
        if groups_left[j] == 0:
            give_away(j)
            plan(n + DELAY, False, lambda m: add_up(j))

    def first_rows(n, g):
        select(0, g)
        plan(n + DELAY, True, lambda m: multiply(m, 0, g))
        plan(n + 3 * DELAY, True, lambda m: multiply(m, 3, g))

    def more_rows(n, j, g):
        select(j, g)
        multiply(n, j, g)

    for g in range(GROUPS):
        plan(ready[(0, g)], False, lambda m, g=g: first_rows(m, g))
        for j in (1, 2):
            plan(ready[(j, g)], True, lambda m, j=j, g=g: more_rows(m, j, g))

    def run_one(n, anything=False):
        for spot, (least, _, needs, call) in enumerate(todo):
            if anything or (least <= n and (opened or not needs)):
                todo.pop(spot)
                call(n)
                return

    prepared = 0
    opened = False
    y_waited = set()
    for n, (now, c, ds, dl, via, onward) in enumerate(log):
        part, _, _, rows, cols, _ = CHUNKS[c]
        src = chip(xs + ds, zl + dl)
        if part == META:
            here = bufm.at[src]
        else:
            here = buf.at[part, src, rows[0] : rows[1], cols[0] : cols[1]]
        origin = here
        if via is None:
            if part == 0:
                origin = g_ref.at[rows[0] : rows[1], cols[0] : cols[1]]
            elif part != META and part not in y_waited:
                y_waited.add(part)
                arrived(buf.at[part, e], yrecv.at[part - 1])
                if part == 1:
                    y_copies[1].start()
        else:
            arrived(here, crecv.at[c, (ds % NS) * NL + dl % NL])
        for link in onward:
            step_s, step_l = SHIFT[link]
            spot = ((ds + step_s) % NS) * NL + (dl + step_l) % NL
            copy = remote(
                origin, here, csend.at[LINKS.index(link), sent[link]], crecv.at[c, spot],
                (q, near[link], t),
            )
            copy.start()
            sent[link] += 1
            sends.append(copy)
        if n == 2:
            for j in range(4):
                for k in range(2):
                    w_copies(j, k, "start")
        while prepared < GROUPS and ready[(META, prepared)] <= n:
            prepare(prepared)
            prepared += 1
        if not opened and now >= FIRST_TASK:
            opened = True
            w_arrive()
        run_one(n)
    while todo:
        run_one(len(log), True)

    for k in range(1, NL):
        arrived(p1.at[:, 0], s1recv.at[k])
    line = []
    for k in range(1, NS):
        to = lax.rem(xs + k, NS)
        copy = remote(
            p1.at[to], scin.at[xs], s2send.at[k - 1], s2recv.at[k - 1], (q, chip(xs + k, zl), t)
        )
        copy.start()
        line.append(copy)
    scin[xs] = p1[xs]
    for copy in line:
        copy.wait_recv()
    chosen = jnp.zeros((8, 128), f32)
    for owner in range(32):
        value = scin[owner % NS, owner // NS]
        chosen += jnp.where(routes_ref[...] == owner, value, 0.0)
    gall[t] = chosen
    for k in range(1, NT):
        copy = remote(
            gall.at[t], gall.at[t], tsend.at[k - 1], trecv.at[k - 1], (q, e, lax.rem(t + k, NT))
        )
        copy.start()
        line.append(copy)
    for copy in line[NS - 1 :]:
        copy.wait_recv()
    total = gall[0]
    for k in range(1, NT):
        total += gall[k]
    gp_ref[...] = total

    for copy in line:
        copy.wait_send()
    for copy in sends:
        copy.wait_send()
    for copy in y_copies:
        copy.wait_send()
    for j in range(4):
        for k in range(2):
            w_copies(j, k, "wait")
    w_relayed()
    for g in range(GROUPS):
        for k in range(2):
            wgt_copy(g, k).wait_send()
            row_copy(g, k).wait_send()
            back_copy(g, k).wait_send()
        if g == 4:
            score_copy(4, 1).wait_send()
        elif g > 0:
            score_copy(g, 1).wait_send()
            score_copy(g, -1).wait_send()
    for j in range(4):
        for k in range(2):
            @pl.when(slice_of(j, t) // 4 != q)
            def _():
                hand(j, k).wait_send()

            @pl.when(slice_of(j, t) // 4 == q)
            def _():
                forward(j, k).wait_send()

            @pl.when(slice_of(j, pair) // 4 == q)
            def _():
                arrived(fams[k]["res"].at[j], frecv.at[j, k])


def owner_kernel(grad_out, routes, probs, vision, down_text, down_vision, pre_text, pre_vision):
    f32, bf16 = jnp.float32, jnp.bfloat16
    ft, fv = pre_text.shape[-1], pre_vision.shape[-1]
    vmem = pl.BlockSpec(memory_space=pltpu.VMEM)
    dma = pltpu.SemaphoreType.DMA
    like = jax.ShapeDtypeStruct

    def two(shape, kind):
        return [pltpu.VMEM(shape(f), kind) for f in (ft, fv)]

    return pl.pallas_call(
        body,
        out_shape=(
            like(pre_text.shape, bf16), like(pre_vision.shape, bf16),
            like(down_text.shape, bf16), like(down_vision.shape, bf16),
            like((8, 128), f32),
        ),
        in_specs=[vmem] * 8,
        out_specs=(vmem,) * 5,
        scratch_shapes=[
            pltpu.VMEM((3, 32, 128, 512), bf16), pltpu.VMEM((32, 64, 128), bf16),
            *two(lambda f: (256, 512), bf16), *two(lambda f: (1024, 512), bf16),
            *two(lambda f: (1024, 512), bf16), *two(lambda f: (2, 4, f, 512), bf16),
            *two(lambda f: (1024, f), bf16), *two(lambda f: (1024, f), bf16),
            *two(lambda f: (1024, f), f32), *two(lambda f: (1024, f), f32),
            *two(lambda f: (1024, f), bf16), *two(lambda f: (1024, f), bf16),
            *two(lambda f: (2, 4, f, 512), f32), *two(lambda f: (4, 2, f, 512), bf16),
            *two(lambda f: (4, 2, f, 512), bf16), *two(lambda f: (4, f, 512), bf16),
            pltpu.VMEM((32, 2 * SLOT, 128), bf16), pltpu.VMEM((2, 32, SLOT, 128), f32),
            *two(lambda f: (SLOT, f), f32),
            pltpu.VMEM((32, 1, 128), f32), pltpu.VMEM((NS, NL, 1, 128), f32),
            pltpu.VMEM((NS, NL, 1, 128), f32), pltpu.VMEM((NT, 8, 128), f32),
            dma((2,)), dma((3,)), dma((4, 96)), dma((len(CHUNKS), 32)),
            dma((2, 4, 2)), dma((2, 4, 2)), dma((4, 2)),
            dma((5, 2)), dma((5, 2)), dma((5, 2)), dma((5, 2)), dma((5, 2)), dma((5, 2)),
            dma((4, 2)), dma((4, 2)), dma((4, 2)), dma((4, 2)),
            dma((NL,)), dma((NL,)), dma((NS - 1,)), dma((NS - 1,)),
            dma((NT - 1,)), dma((NT - 1,)),
        ],
        compiler_params=pltpu.CompilerParams(
            collective_id=0, has_side_effects=True, vmem_limit_bytes=60 * 1024 * 1024
        ),
        cost_estimate=pl.CostEstimate(
            flops=7_000_000_000, bytes_accessed=10_000_000, transcendentals=2_000_000
        ),
    )(grad_out, routes, probs, vision, down_text, down_vision, pre_text, pre_vision)


def on_device(grad_out, routes, probs, vision, pre_text, pre_vision, down_text, down_vision):
    gpt, gpv, gdt, gdv, gp = owner_kernel(
        grad_out, routes.T, probs.T.astype(jnp.float32), vision[None, :],
        down_text, down_vision, pre_text, pre_vision,
    )
    return gpt, gpv, gdt, gdv, gp.T


def solution(mesh):
    in_specs = (
        P(("dp", "expert"), "tensor"),
        P(("dp", "expert"), None),
        P(("dp", "expert"), None),
        P(("dp", "expert")),
        P("dp", "expert", None, None, None, "tensor"),
        P("dp", "expert", None, None, None, "tensor"),
        P("expert", "tensor", "dp"),
        P("expert", "tensor", "dp"),
    )
    out_specs = (
        P("dp", "expert", None, None, None, "tensor"),
        P("dp", "expert", None, None, None, "tensor"),
        P("expert", "tensor", "dp"),
        P("expert", "tensor", "dp"),
        P(("dp", "expert"), None),
    )
    return jax.shard_map(
        on_device, mesh=mesh, in_specs=in_specs, out_specs=out_specs, check_vma=False
    )
```

```python
import heapq

import jax
import jax.numpy as jnp
from jax import lax
from jax.experimental import pallas as pl
from jax.experimental.pallas import tpu as pltpu
from jax.sharding import PartitionSpec as P

MESH = pl.DeviceIdType.MESH
NL, NS, NT = 8, 4, 8
SLOT = 32
CAP = 28
LINKS = ("l+", "l-", "s+", "s-")
SHIFT = {"l+": (0, -1), "l-": (0, 1), "s+": (-1, 0), "s-": (1, 0)}
META = 3
CHUNKS = (
    (META, "s", 0, (0, 64), (0, 128), 0.0),
    (0, "s", 0, (0, 48), (0, 512), 0.0),
    (0, "l", 1, (48, 128), (0, 512), 0.0),
    (1, "s", 1, (0, 48), (0, 512), 3.0),
    (1, "l", 0, (48, 128), (0, 512), 3.0),
    (2, "s", 0, (0, 48), (0, 256), 4.5),
    (2, "s", 1, (0, 48), (256, 512), 4.5),
    (2, "l", 0, (48, 128), (0, 256), 4.5),
    (2, "l", 1, (48, 128), (256, 512), 4.5),
)
FIRST_TASK = 9.0
DELAY = 14
ROW_DELAY = 42
W_STEP = 4
GROUPS = 5
BASE = {0: 0, 1: 128, 2: 384, 3: 640, 4: 896}
BLOCKS = {0: 4, 1: 8, 2: 8, 3: 8, 4: 4}


def hops(first, odd, ds, dl, via):
    right, left = (4, 3) if odd == 0 else (3, 4)
    up, down = (2, 1) if odd == 0 else (1, 2)
    out = []
    along_l = (via == "l+" and -dl < right) or (via == "l-" and dl < left)
    along_s = (via == "s+" and -ds < up) or (via == "s-" and ds < down)
    if first == "s":
        if dl == 0:
            if ds == 0:
                out += ["s+", "s-"]
            elif along_s:
                out.append(via)
            out += ["l+", "l-"]
        elif along_l:
            out.append(via)
    else:
        if ds == 0:
            if dl == 0:
                out += ["l+", "l-"]
            elif along_l:
                out.append(via)
            out += ["s+", "s-"]
        elif along_s:
            out.append(via)
    return out


def schedule():
    free = {link: 0.0 for link in LINKS}
    queue, count, log = [], 0, []
    for c, chunk in enumerate(CHUNKS):
        heapq.heappush(queue, (chunk[5], count, c, 0, 0, None))
        count += 1
    while queue:
        now, _, c, ds, dl, via = heapq.heappop(queue)
        _, first, odd, rows, cols, _ = CHUNKS[c]
        size = (rows[1] - rows[0]) * (cols[1] - cols[0]) / (128 * 512)
        onward = hops(first, odd, ds, dl, via)
        log.append((now, c, ds, dl, via, onward))
        for link in onward:
            free[link] = max(now, free[link]) + size
            step_s, step_l = SHIFT[link]
            item = (free[link] + 0.4, count, c, ds + step_s, dl + step_l, link)
            heapq.heappush(queue, item)
            count += 1
    return log


def slice_of(j, t):
    odd = lax.rem(t, 2)
    mate = lax.rem(t + NT + 2 * odd - 1, NT)
    if j == 0:
        return t
    if j == 1:
        return lax.rem(t + NT + 3 - 6 * odd, NT)
    if j == 2:
        return slice_of(1, mate)
    return mate


def body(
    g_ref, routes_ref, probs_ref, vision_ref, wt_ref, wv_ref, pt_ref, pv_ref,
    gpt_ref, gpv_ref, gdt_ref, gdv_ref, gp_ref,
    buf, bufm, rows_t, rows_v, srow_t, srow_v, prow_t, prow_v, wb_t, wb_v,
    wgt_t, wgt_v, pwgt_t, pwgt_v, bown_t, bown_v, bpair_t, bpair_v,
    bsend_t, bsend_v, brecv_t, brecv_v, acc_t, acc_v, give_t, give_v,
    grecv_t, grecv_v, res_t, res_v, sel, sw, tmp_t, tmp_v, scs, p1, scin, gall,
    ysend, yrecv, csend, crecv, wsend, wrecv, wback, hsend, hrecv, rsend, rrecv,
    bsem, brsem, gsend, grsem, fsend, frecv, s1send, s1recv, s2send, s2recv,
    tsend, trecv,
):
    f32, bf16 = jnp.float32, jnp.bfloat16
    q = lax.axis_index("dp")
    e = lax.axis_index("expert")
    t = lax.axis_index("tensor")
    zl, xs = e // NS, lax.rem(e, NS)
    pair = t + 1 - 2 * lax.rem(t, 2)
    mate = slice_of(3, t)
    far = slice_of(1, t)
    other = 1 - q

    def chip(s_, l_):
        return lax.rem(l_ + 2 * NL, NL) * NS + lax.rem(s_ + 2 * NS, NS)

    near = {
        "l+": chip(xs, zl + 1), "l-": chip(xs, zl - 1),
        "s+": chip(xs + 1, zl), "s-": chip(xs - 1, zl),
    }

    barrier = pltpu.get_barrier_semaphore()

    def greet(where):
        pl.semaphore_signal(barrier, inc=1, device_id=where, device_id_type=MESH)

    for k in range(1, NL):
        greet((q, chip(xs, zl + k), t))
    for k in range(1, NS):
        greet((q, chip(xs + k, zl), t))
    for k in range(1, NT):
        greet((q, e, lax.rem(t + k, NT)))
    greet((other, e, t))
    pl.semaphore_wait(barrier, NL + NS + NT - 3 + 1)

    def remote(src, dst, send, recv, where):
        return pltpu.make_async_remote_copy(
            src_ref=src, dst_ref=dst, send_sem=send, recv_sem=recv,
            device_id=where, device_id_type=MESH,
        )

    def arrived(ref, sem):
        pltpu.make_async_copy(ref, ref, sem).wait()

    y_copies = (
        remote(g_ref, buf.at[1, e], ysend.at[0], yrecv.at[0], (q, e, far)),
        remote(buf.at[1, e], buf.at[2, e], ysend.at[1], yrecv.at[1], (q, e, mate)),
    )
    y_copies[0].start()
    own = pltpu.make_async_copy(g_ref, buf.at[0, e], yrecv.at[2])
    own.start()

    expert = lax.broadcasted_iota(jnp.int32, (32, 128), 0)
    weight = jnp.zeros((32, 128), f32)
    probs = probs_ref[...].astype(f32)
    for k in range(8):
        named = routes_ref[k : k + 1, :] == expert
        weight += jnp.where(named, probs[k : k + 1, :], 0.0)
    image = vision_ref[...] == 1
    bufm[e, 0:32] = jnp.where(image, 0.0, weight).astype(bf16)
    bufm[e, 32:64] = jnp.where(image, weight, 0.0).astype(bf16)
    tmp_t[...] = jnp.zeros_like(tmp_t)
    tmp_v[...] = jnp.zeros_like(tmp_v)
    own.wait()

    w_fams = ((wt_ref, wb_t), (wv_ref, wb_v))

    def w_cols(u):
        return pl.ds(pl.multiple_of(lax.rem(u, 4) * 512, 512), 512)

    def w_copies(j, k, action):
        src, box = w_fams[k]
        u = slice_of(j, t)
        v = slice_of(j, pair)

        @pl.when(u // 4 == q)
        def _():
            here = src.at[0, :, w_cols(u)]
            there = remote(here, box.at[0, j], wsend.at[0, j, k], wrecv.at[0, j, k], (other, e, t))
            if action == "start":
                pltpu.make_async_copy(here, box.at[0, j], wrecv.at[0, j, k]).start()
                there.start()
            else:
                there.wait_send()

        @pl.when(v // 4 == q)
        def _():
            there = remote(
                src.at[0, :, w_cols(v)], box.at[1, j], wsend.at[1, j, k], wrecv.at[1, j, k],
                (q, e, pair),
            )
            if action == "start":
                there.start()
            else:
                there.wait_send()

    def w_relay(j, k):
        box = w_fams[k][1]
        return remote(
            box.at[1, j], box.at[1, j], wback.at[j, k], wrecv.at[1, j, k], (other, e, t)
        )

    def w_arrive():
        for j in range(4):
            for k in range(2):
                arrived(w_fams[k][1].at[1, j], wrecv.at[1, j, k])

                @pl.when(slice_of(j, t) // 4 == q)
                def _():
                    w_relay(j, k).start()

        for j in range(4):
            for k in range(2):
                arrived(w_fams[k][1].at[0, j], wrecv.at[0, j, k])

    def w_relayed():
        for j in range(4):
            for k in range(2):
                @pl.when(slice_of(j, t) // 4 == q)
                def _():
                    w_relay(j, k).wait_send()

    upper = (
        lax.broadcasted_iota(jnp.int32, (128, 128), 0)
        < lax.broadcasted_iota(jnp.int32, (128, 128), 1)
    ).astype(bf16)

    def block_of(g, i):
        sign = 1 - 2 * (i // 4)
        return chip(xs + lax.rem(i, 4), zl + g * sign)

    def place(g, i):
        return pl.ds(pl.multiple_of(BASE[g] + i * SLOT, SLOT), SLOT)

    def span(g):
        return slice(BASE[g], BASE[g] + BLOCKS[g] * SLOT)

    def pieces(ref, s):
        gate = ref[0, 0, 0, s].astype(f32)
        up = ref[0, 0, 1, s].astype(f32)
        return gate, up, jax.nn.sigmoid(gate)

    fams = (
        dict(pre=pt_ref, grad=gpt_ref, rows=rows_t, srow=srow_t, prow=prow_t, wb=wb_t, wgt=wgt_t,
             pwgt=pwgt_t, bown=bown_t, bpair=bpair_t, bsend=bsend_t, brecv=brecv_t, acc=acc_t,
             give=give_t, grecv=grecv_t, res=res_t, out=gdt_ref, tmp=tmp_t),
        dict(pre=pv_ref, grad=gpv_ref, rows=rows_v, srow=srow_v, prow=prow_v, wb=wb_v, wgt=wgt_v,
             pwgt=pwgt_v, bown=bown_v, bpair=bpair_v, bsend=bsend_v, brecv=brecv_v, acc=acc_v,
             give=give_v, grecv=grecv_v, res=res_v, out=gdv_ref, tmp=tmp_v),
    )

    def wgt_copy(g, k):
        at = pl.ds(BASE[g], BLOCKS[g] * SLOT)
        return remote(
            fams[k]["wgt"].at[at], fams[k]["pwgt"].at[at], hsend.at[g, k], hrecv.at[g, k],
            (q, e, pair),
        )

    def prepare(g):
        def step(i, carry):
            src = block_of(g, i)
            table = bufm[src].astype(f32)
            row = lax.broadcasted_iota(jnp.int32, (64, 128), 0)
            found = [
                jnp.sum(jnp.where(row == k * 32 + e, table, 0.0), axis=0, keepdims=True)
                for k in range(2)
            ]
            sub = lax.broadcasted_iota(jnp.int32, (8, 128), 0)
            both = jnp.where(sub == 0, found[0], jnp.where(sub == 1, found[1], 0.0))
            rank = jnp.dot((both > 0.0).astype(bf16), upper, preferred_element_type=f32)
            want = lax.broadcasted_iota(jnp.int32, (SLOT, 128), 0).astype(f32)
            for k, fam in enumerate(fams):
                hit = jnp.logical_and(want == rank[k : k + 1], found[k] > 0.0)
                pick = jnp.where(hit, 1.0, 0.0)
                scale = jnp.sum(pick * found[k], axis=1, keepdims=True)
                sw[k, src] = jnp.broadcast_to(scale, (SLOT, 128))
                sel[src, k * SLOT : (k + 1) * SLOT] = pick.astype(bf16)
                gate, up, sig = pieces(fam["pre"], src)
                fam["tmp"][0:CAP, :] = gate * sig * up
                fam["wgt"][place(g, i)] = (scale * fam["tmp"][...]).astype(bf16)
            return carry

        lax.fori_loop(0, BLOCKS[g], step, 0)
        for k in range(2):
            wgt_copy(g, k).start()

    def row_copy(g, k):
        at = pl.ds(BASE[g], BLOCKS[g] * SLOT)
        return remote(
            fams[k]["srow"].at[at], fams[k]["prow"].at[at], rsend.at[g, k], rrecv.at[g, k],
            (q, e, mate),
        )

    def back_copy(g, k):
        at = pl.ds(BASE[g], BLOCKS[g] * SLOT)
        return remote(
            fams[k]["bsend"].at[at], fams[k]["brecv"].at[at], bsem.at[g, k], brsem.at[g, k],
            (q, e, pair),
        )

    nt_dims = (((1,), (1,)), ((), ()))
    tn_dims = (((0,), (0,)), ((), ()))
    waited = set()
    begun = set()
    added = {g: 0 for g in range(GROUPS)}

    def select(j, g):
        def step(i, carry):
            src = block_of(g, i)
            got = jnp.dot(sel[src], buf[j, src], preferred_element_type=f32).astype(bf16)
            for k, fam in enumerate(fams):
                spot = pl.ds(pl.multiple_of(i * SLOT, SLOT), SLOT)
                fam["rows"][spot] = got[k * SLOT : (k + 1) * SLOT]
            return carry

        lax.fori_loop(0, BLOCKS[g], step, 0)

    def select_shared(g, i):
        got = jnp.dot(sel[block_of(g, i)], buf[0, block_of(g, i)], preferred_element_type=f32)
        at = pl.ds(BASE[g] + i * SLOT, SLOT)
        for k, fam in enumerate(fams):
            fam["srow"][at] = got[k * SLOT : (k + 1) * SLOT].astype(bf16)
            remote(
                fam["srow"].at[at], fam["prow"].at[at], rsend.at[g, k], rrecv.at[g, k],
                (q, e, mate),
            ).start()

    def products(j, g):
        m = BLOCKS[g] * SLOT
        if g not in waited:
            waited.add(g)
            for k in range(2):
                wgt_copy(g, k).wait_recv()
        if j == 3:
            for k in range(2):
                row_copy(g, k).wait_recv()
        final = added[g] == 3
        for k, fam in enumerate(fams):
            rows = {0: fam["srow"], 3: fam["prow"]}.get(j)
            rows = fam["rows"][0:m] if rows is None else rows[span(g)]
            theirs = lax.dot_general(rows, fam["wb"][1, j], nt_dims, preferred_element_type=f32)
            if added[g]:
                theirs += fam["bpair"][span(g)]
            if final:
                fam["bsend"][span(g)] = theirs.astype(bf16)
                back_copy(g, k).start()
            else:
                fam["bpair"][span(g)] = theirs
        for k, fam in enumerate(fams):
            rows = {0: fam["srow"], 3: fam["prow"]}.get(j)
            rows = fam["rows"][0:m] if rows is None else rows[span(g)]
            ours = lax.dot_general(rows, fam["wb"][0, j], nt_dims, preferred_element_type=f32)
            if added[g]:
                ours += fam["bown"][span(g)]
            fam["bown"][span(g)] = ours
            for n, wgt in enumerate((fam["wgt"], fam["pwgt"])):
                add = lax.dot_general(wgt[span(g)], rows, tn_dims, preferred_element_type=f32)
                if j in begun:
                    fam["acc"][n, j] += add
                else:
                    fam["acc"][n, j] = add
        added[g] += 1
        begun.add(j)
        return final

    def hand(j, k):
        fam = fams[k]
        return remote(
            fam["give"].at[j], fam["grecv"].at[j], gsend.at[j, k], grsem.at[j, k], (other, e, t)
        )

    def forward(j, k):
        fam = fams[k]
        return remote(
            fam["res"].at[j], fam["out"].at[0, :, w_cols(slice_of(j, t))], fsend.at[j, k],
            frecv.at[j, k], (q, e, pair),
        )

    def give_away(j):
        @pl.when(slice_of(j, t) // 4 != q)
        def _():
            for k, fam in enumerate(fams):
                fam["give"][j] = fam["acc"][:, j].astype(bf16)
                hand(j, k).start()

    def add_up(j):
        @pl.when(slice_of(j, t) // 4 == q)
        def _():
            for k, fam in enumerate(fams):
                hand(j, k).wait_recv()
                for n in (1, 0):
                    here = fam["acc"][n, j].astype(bf16).astype(f32)
                    total = (here + fam["grecv"][j, n].astype(f32)).astype(bf16)
                    if n == 1:
                        fam["res"][j] = total
                        forward(j, k).start()
                    else:
                        fam["out"][0, :, w_cols(slice_of(j, t))] = total

    def score_copy(g, sign):
        to = lax.rem(zl + sign * g + NL, NL)
        return remote(
            scs.at[pl.ds(to * NS, NS)], p1.at[:, zl], s1send.at[(sign * g) % NL],
            s1recv.at[(-sign * g) % NL], (q, chip(xs, zl + sign * g), t),
        )

    def finish(g):
        for k in range(2):
            back_copy(g, k).wait_recv()

        def step(i, carry):
            src = block_of(g, i)
            total = jnp.zeros((1, 128), f32)
            for k, fam in enumerate(fams):
                spot = place(g, i)
                back = (fam["bown"][spot] + fam["brecv"][spot].astype(f32))[0:CAP]
                gate, up, sig = pieces(fam["pre"], src)
                scaled = sw[k, src][0:CAP, 0:1] * back
                grad = fam["grad"]
                grad[0, 0, 0, src] = (scaled * up * sig * (1.0 + gate * (1.0 - sig))).astype(bf16)
                grad[0, 0, 1, src] = (scaled * gate * sig).astype(bf16)
                score = jnp.sum(gate * sig * up * back, axis=1, keepdims=True)
                pick = sel[src, k * SLOT : (k + 1) * SLOT].astype(f32)
                total += jnp.sum(pick[0:CAP] * score, axis=0, keepdims=True)
            scs[src] = total
            return carry

        lax.fori_loop(0, BLOCKS[g], step, 0)
        if g == 0:
            p1[:, zl] = scs[pl.ds(zl * NS, NS)]
        elif g == 4:
            score_copy(4, 1).start()
        else:
            score_copy(g, 1).start()
            score_copy(g, -1).start()

    log = schedule()
    ready, block_ready = {}, {}
    for n, (now, c, ds, dl, via, onward) in enumerate(log):
        ready[(CHUNKS[c][0], min(dl % NL, -dl % NL))] = n
        if CHUNKS[c][0] == 0:
            block_ready[(ds % NS, dl % NL)] = n
    sent = {link: 0 for link in LINKS}
    sends = []
    todo = []
    groups_left = {j: GROUPS for j in range(4)}

    def plan(n, needs, call):
        todo.append((n, len(todo) + planned[0], needs, call))
        planned[0] += 1
        todo.sort(key=lambda item: item[:2])

    planned = [0]

    def multiply(n, j, g):
        if products(j, g):
            plan(n + DELAY, False, lambda m: finish(g))
        groups_left[j] -= 1
        if groups_left[j] == 0:
            give_away(j)
            plan(n + DELAY, False, lambda m: add_up(j))

    blocks_left = dict(BLOCKS)

    def first_rows(n, g, i):
        select_shared(g, i)
        blocks_left[g] -= 1
        if blocks_left[g] == 0:
            plan(n + DELAY, True, lambda m: multiply(m, 0, g))
            plan(n + ROW_DELAY, True, lambda m: multiply(m, 3, g))

    def more_rows(n, j, g):
        select(j, g)
        multiply(n, j, g)

    for g in range(GROUPS):
        for i in range(BLOCKS[g]):
            dl = g if i < 4 else -g
            least = max(block_ready[(i % 4, dl % NL)], ready[(META, g)])
            plan(least, False, lambda m, g=g, i=i: first_rows(m, g, i))
        for j in (1, 2):
            plan(ready[(j, g)], True, lambda m, j=j, g=g: more_rows(m, j, g))

    def run_one(n, anything=False):
        for spot, (least, _, needs, call) in enumerate(todo):
            if anything or (least <= n and (opened or not needs)):
                todo.pop(spot)
                call(n)
                return

    prepared = 0
    opened = False
    y_waited = set()
    w_begun = 0
    for n, (now, c, ds, dl, via, onward) in enumerate(log):
        part, _, _, rows, cols, _ = CHUNKS[c]
        src = chip(xs + ds, zl + dl)
        if part == META:
            here = bufm.at[src]
        else:
            here = buf.at[part, src, rows[0] : rows[1], cols[0] : cols[1]]
        origin = here
        if via is None:
            if part == 0:
                origin = g_ref.at[rows[0] : rows[1], cols[0] : cols[1]]
            elif part != META and part not in y_waited:
                y_waited.add(part)
                arrived(buf.at[part, e], yrecv.at[part - 1])
                if part == 1:
                    y_copies[1].start()
        else:
            arrived(here, crecv.at[c, (ds % NS) * NL + dl % NL])
        for link in onward:
            step_s, step_l = SHIFT[link]
            spot = ((ds + step_s) % NS) * NL + (dl + step_l) % NL
            copy = remote(
                origin, here, csend.at[LINKS.index(link), sent[link]], crecv.at[c, spot],
                (q, near[link], t),
            )
            copy.start()
            sent[link] += 1
            sends.append(copy)
        if n >= 2 and w_begun < 8 and (n - 2) % W_STEP == 0:
            w_copies(w_begun // 2, w_begun % 2, "start")
            w_begun += 1
        while prepared < GROUPS and ready[(META, prepared)] <= n:
            prepare(prepared)
            prepared += 1
        if not opened and now >= FIRST_TASK:
            opened = True
            w_arrive()
        run_one(n)
    while todo:
        run_one(len(log), True)

    for k in range(1, NL):
        arrived(p1.at[:, 0], s1recv.at[k])
    line = []
    for k in range(1, NS):
        to = lax.rem(xs + k, NS)
        copy = remote(
            p1.at[to], scin.at[xs], s2send.at[k - 1], s2recv.at[k - 1], (q, chip(xs + k, zl), t)
        )
        copy.start()
        line.append(copy)
    scin[xs] = p1[xs]
    for copy in line:
        copy.wait_recv()
    chosen = jnp.zeros((8, 128), f32)
    for owner in range(32):
        value = scin[owner % NS, owner // NS]
        chosen += jnp.where(routes_ref[...] == owner, value, 0.0)
    gall[t] = chosen
    for k in range(1, NT):
        copy = remote(
            gall.at[t], gall.at[t], tsend.at[k - 1], trecv.at[k - 1], (q, e, lax.rem(t + k, NT))
        )
        copy.start()
        line.append(copy)
    for copy in line[NS - 1 :]:
        copy.wait_recv()
    total = gall[0]
    for k in range(1, NT):
        total += gall[k]
    gp_ref[...] = total

    for copy in line:
        copy.wait_send()
    for copy in sends:
        copy.wait_send()
    for copy in y_copies:
        copy.wait_send()
    for j in range(4):
        for k in range(2):
            w_copies(j, k, "wait")
    w_relayed()
    for g in range(GROUPS):
        for k in range(2):
            wgt_copy(g, k).wait_send()
            row_copy(g, k).wait_send()
            back_copy(g, k).wait_send()
        if g == 4:
            score_copy(4, 1).wait_send()
        elif g > 0:
            score_copy(g, 1).wait_send()
            score_copy(g, -1).wait_send()
    for j in range(4):
        for k in range(2):
            @pl.when(slice_of(j, t) // 4 != q)
            def _():
                hand(j, k).wait_send()

            @pl.when(slice_of(j, t) // 4 == q)
            def _():
                forward(j, k).wait_send()

            @pl.when(slice_of(j, pair) // 4 == q)
            def _():
                arrived(fams[k]["res"].at[j], frecv.at[j, k])


def owner_kernel(grad_out, routes, probs, vision, down_text, down_vision, pre_text, pre_vision):
    f32, bf16 = jnp.float32, jnp.bfloat16
    ft, fv = pre_text.shape[-1], pre_vision.shape[-1]
    vmem = pl.BlockSpec(memory_space=pltpu.VMEM)
    dma = pltpu.SemaphoreType.DMA
    like = jax.ShapeDtypeStruct

    def two(shape, kind):
        return [pltpu.VMEM(shape(f), kind) for f in (ft, fv)]

    return pl.pallas_call(
        body,
        out_shape=(
            like(pre_text.shape, bf16), like(pre_vision.shape, bf16),
            like(down_text.shape, bf16), like(down_vision.shape, bf16),
            like((8, 128), f32),
        ),
        in_specs=[vmem] * 8,
        out_specs=(vmem,) * 5,
        scratch_shapes=[
            pltpu.VMEM((3, 32, 128, 512), bf16), pltpu.VMEM((32, 64, 128), bf16),
            *two(lambda f: (256, 512), bf16), *two(lambda f: (1024, 512), bf16),
            *two(lambda f: (1024, 512), bf16), *two(lambda f: (2, 4, f, 512), bf16),
            *two(lambda f: (1024, f), bf16), *two(lambda f: (1024, f), bf16),
            *two(lambda f: (1024, f), f32), *two(lambda f: (1024, f), f32),
            *two(lambda f: (1024, f), bf16), *two(lambda f: (1024, f), bf16),
            *two(lambda f: (2, 4, f, 512), f32), *two(lambda f: (4, 2, f, 512), bf16),
            *two(lambda f: (4, 2, f, 512), bf16), *two(lambda f: (4, f, 512), bf16),
            pltpu.VMEM((32, 2 * SLOT, 128), bf16), pltpu.VMEM((2, 32, SLOT, 128), f32),
            *two(lambda f: (SLOT, f), f32),
            pltpu.VMEM((32, 1, 128), f32), pltpu.VMEM((NS, NL, 1, 128), f32),
            pltpu.VMEM((NS, NL, 1, 128), f32), pltpu.VMEM((NT, 8, 128), f32),
            dma((2,)), dma((3,)), dma((4, 96)), dma((len(CHUNKS), 32)),
            dma((2, 4, 2)), dma((2, 4, 2)), dma((4, 2)),
            dma((5, 2)), dma((5, 2)), dma((5, 2)), dma((5, 2)), dma((5, 2)), dma((5, 2)),
            dma((4, 2)), dma((4, 2)), dma((4, 2)), dma((4, 2)),
            dma((NL,)), dma((NL,)), dma((NS - 1,)), dma((NS - 1,)),
            dma((NT - 1,)), dma((NT - 1,)),
        ],
        compiler_params=pltpu.CompilerParams(
            collective_id=0, has_side_effects=True, vmem_limit_bytes=60 * 1024 * 1024
        ),
        cost_estimate=pl.CostEstimate(
            flops=7_000_000_000, bytes_accessed=10_000_000, transcendentals=2_000_000
        ),
    )(grad_out, routes, probs, vision, down_text, down_vision, pre_text, pre_vision)


def on_device(grad_out, routes, probs, vision, pre_text, pre_vision, down_text, down_vision):
    gpt, gpv, gdt, gdv, gp = owner_kernel(
        grad_out, routes.T, probs.T, vision[None, :],
        down_text, down_vision, pre_text, pre_vision,
    )
    return gpt, gpv, gdt, gdv, gp.T


def solution(mesh):
    in_specs = (
        P(("dp", "expert"), "tensor"),
        P(("dp", "expert"), None),
        P(("dp", "expert"), None),
        P(("dp", "expert")),
        P("dp", "expert", None, None, None, "tensor"),
        P("dp", "expert", None, None, None, "tensor"),
        P("expert", "tensor", "dp"),
        P("expert", "tensor", "dp"),
    )
    out_specs = (
        P("dp", "expert", None, None, None, "tensor"),
        P("dp", "expert", None, None, None, "tensor"),
        P("expert", "tensor", "dp"),
        P("expert", "tensor", "dp"),
        P(("dp", "expert"), None),
    )
    return jax.shard_map(
        on_device, mesh=mesh, in_specs=in_specs, out_specs=out_specs, check_vma=False
    )
```
